256 devices in a mesh: tm: 4 (over x_lo, core), sx: 8 (over z), sy: 8 (over x_hi, y).
Axes of the slice: x: 4 (x_hi: 2, x_lo: 2; x = x_hi * 2 + x_lo), y: 4, z: 8, core: 2. Of those that a mesh axis runs over, the one named last changes fastest.
Arguments:
- right_side: float32 [4, 16, 64, 128, 128], P('tm', None, 'sx', 'sy'), may hold values from -6 to 6
- current: float32 [4, 16, 64, 128, 128], P('tm', None, 'sx', 'sy'), may hold values from -6 to 6
- classes: int32 [4, 64, 128, 128], P('tm', 'sx', 'sy'), may hold values from 0 to 7
- volume: float32 [8, 16, 16], replicated, may hold values from -0.35 to 12
- face_gain: float32 [8, 6], replicated, may hold values from 0.5 to 2
- time_gain: float32 [8], replicated, may hold values from 0.5 to 2
Outputs:
- smoothed: float32 [4, 16, 64, 128, 128], P('tm', None, 'sx', 'sy')
The draws below stay inside these ranges and needn't reach their ends.
All inputs are finite; a program needn't handle non-finite values.
Results may differ from the reference program's by a relative error of at most 0.0001.
Values sent between devices are 32-bit elements; how exact they have to be, the bound alone decides.
No kernel may reach another device: no remote copies, remote signals or barrier semaphores. Data moves between devices by JAX's collectives and lax.ppermute only.
A program may use at most 64 MiB of HBM per device.

```python
import math
import jax
import jax.numpy as jnp
from jax import lax

NODES = 16
NCLASS = 8
CZ = 128
NT = 4
NX = 64
NY = 128


def draw_volume(key, part):
    key = jax.random.fold_in(key, 11)
    first, second = jax.random.split(key, 2)
    diagonal = jax.random.uniform(first, (NCLASS, NODES), jnp.float32, 6.0, 12.0)
    off = jax.random.uniform(second, (NCLASS, NODES, NODES), jnp.float32, -0.35, 0.35)
    eye = jnp.eye(NODES, dtype=jnp.float32)
    return (off * (1.0 - eye)[None] + diagonal[:, :, None] * eye[None]).astype(jnp.float32)


def plant(drawn, own_key, least, largest):
    place = [jax.random.randint(jax.random.fold_in(own_key, axis), (), 0, length) for axis, length in enumerate(drawn.shape)]
    widest = drawn.shape.index(max(drawn.shape))
    beside = place[:widest] + [(place[widest] + 1) % drawn.shape[widest]] + place[widest + 1:]
    return drawn.at[tuple(place)].set(least).at[tuple(beside)].set(largest)


def block_levels(own_key, shape, cuts, least, high):
    def one(position, shards_of):
        steps = jax.random.uniform(jax.random.fold_in(jax.random.fold_in(own_key, 6), position), (shards_of,), jnp.float32, least / len(cuts), high / len(cuts))
        return jnp.repeat(jnp.exp(steps), shape[position] // shards_of).reshape((-1,) + (1,) * (len(shape) - position - 1))

    factor_of = one(*cuts[0])
    for cut in cuts[1:]:
        factor_of = factor_of * one(*cut)
    return factor_of


def centred(rng, dims, scale, most, shards=(), kind=jnp.bfloat16):
    loudness = block_levels(rng, dims, shards, -0.22, 0.18) if shards else 1.0
    entries = jax.random.normal(rng, dims, jnp.float32) * scale * loudness
    return jnp.minimum(jnp.maximum(entries, -most), most).astype(kind)


def setup_inputs(seed: int = 0) -> dict:
    splits = jax.random.split(jax.random.key(seed), 7)
    return {
        "right_side": centred(splits[0], (NT, NODES, NX, NY, CZ), 1.0, 6.0, ((0, 4), (2, 8), (3, 8)), jnp.float32),
        "current": centred(splits[1], (NT, NODES, NX, NY, CZ), 1.0, 6.0, ((0, 4), (2, 8), (3, 8)), jnp.float32),
        "classes": plant(jax.random.randint(splits[2], (NT, NX, NY, CZ), 0, NCLASS), jax.random.fold_in(splits[2], 1), 0, NCLASS - 1).astype(jnp.int32),
        "volume": draw_volume(jax.random.fold_in(splits[6], 71), 0),
        "face_gain": jnp.clip(jnp.exp(jax.random.uniform(splits[4], (NCLASS, 6), jnp.float32, math.log(0.5), math.log(2.0))), 0.5, 2.0),
        "time_gain": jnp.clip(jnp.exp(jax.random.uniform(splits[5], (NCLASS,), jnp.float32, math.log(0.5), math.log(2.0))), 0.5, 2.0),
    }


def invert_blocks(volume):
    eye = jnp.eye(volume.shape[1], dtype=jnp.float32)
    diagonal = jnp.diagonal(volume, axis1=1, axis2=2)
    approx = eye[None] * (1.0 / diagonal)[:, None, :]
    for step in range(12):
        product = jnp.einsum("cij,cjk->cik", volume, approx, precision=lax.Precision.HIGHEST)
        approx = jnp.einsum("cij,cjk->cik", approx, 2.0 * eye[None] - product, precision=lax.Precision.HIGHEST)
    return approx


def apply_blocks(tables, field, onehot):
    count = tables.shape[0]
    nodes = tables.shape[1]
    stacked = tables.reshape(count * nodes, nodes)
    slabs = []
    for slab in range(field.shape[0]):
        flat = field[slab].reshape(nodes, -1)
        product = jnp.dot(stacked, flat, precision=lax.Precision.HIGHEST, preferred_element_type=jnp.float32)
        product = product.reshape(count, nodes, -1)
        picked = jnp.sum(product * onehot[:, slab].reshape(count, 1, -1), axis=0)
        slabs.append(picked.reshape(field.shape[1:]))
    return jnp.stack(slabs)


def coupling(field8, gains, hcell):
    xplus = jnp.roll(field8[:, :, 0], -1, axis=4)
    xminus = jnp.roll(field8[:, :, 1], 1, axis=4)
    yplus = jnp.roll(field8[:, :, :, 0], -1, axis=5)
    yminus = jnp.roll(field8[:, :, :, 1], 1, axis=5)
    zplus = jnp.roll(field8[:, :, :, :, 0], -1, axis=6)
    zminus = jnp.roll(field8[:, :, :, :, 1], 1, axis=6)
    upper = field8[:, 1]
    before = jnp.concatenate([jnp.zeros_like(upper[:1]), upper[:-1]], axis=0)
    return assemble(xminus, xplus, yminus, yplus, zminus, zplus, before, gains, hcell)


def assemble(xminus, xplus, yminus, yplus, zminus, zplus, before, gains, hcell):
    spread = lambda g: g[:, None, None, None]
    along_x = jnp.stack([spread(gains[0]) * xminus, spread(gains[1]) * xplus], axis=2)
    along_y = jnp.stack([spread(gains[2]) * yminus, spread(gains[3]) * yplus], axis=3)
    along_z = jnp.stack([spread(gains[4]) * zminus, spread(gains[5]) * zplus], axis=4)
    timed = spread(hcell) * before
    along_t = jnp.stack([timed, jnp.zeros_like(timed)], axis=1)
    return along_x + along_y + along_z + along_t


def reference(right_side, current, classes, volume, face_gain, time_gain):
    count = volume.shape[0]
    labels = jnp.arange(count, dtype=jnp.int32).reshape(count, 1, 1, 1, 1)
    onehot = (classes[None] == labels).astype(jnp.float32)
    gains = jnp.einsum("ck,ctxyz->ktxyz", face_gain, onehot, precision=lax.Precision.HIGHEST)
    hcell = jnp.einsum("c,ctxyz->txyz", time_gain, onehot, precision=lax.Precision.HIGHEST)
    inverse = invert_blocks(volume)
    shape = current.shape
    split = (shape[0], 2, 2, 2, 2) + shape[2:]
    field = current
    for sweep in range(2):
        field8 = field.reshape(split)
        image = apply_blocks(volume, field, onehot) - coupling(field8, gains, hcell).reshape(shape)
        field = field + 0.7 * apply_blocks(inverse, right_side - image, onehot)
    return field
```

```python
import functools
import jax
import jax.numpy as jnp
from jax import lax
from jax.experimental import pallas as pl
from jax.experimental.pallas import tpu as pltpu
from jax.sharding import PartitionSpec as P

F32 = jnp.float32
BF16 = jnp.bfloat16
DAMP = 0.7
VMEM = pl.BlockSpec(memory_space=pltpu.VMEM)
SMEM = pl.BlockSpec(memory_space=pltpu.SMEM)
PARAMS = pltpu.CompilerParams(vmem_limit_bytes=40 * 1024 * 1024)


def bit_of(shape, dim, m):
    return (lax.broadcasted_iota(jnp.int32, shape, dim) & m) != 0


def split2(v):
    hi = v.astype(BF16)
    lo = (v - hi.astype(F32)).astype(BF16)
    return hi, lo


def pack_faces(lower, upper, m, want):
    keep = bit_of(lower.shape, 0, m) == want
    by = m if not want else 8 - m
    return jnp.where(keep, lower, pltpu.roll(upper, by, 0))


def unpack_faces(msg, m, want):
    by = 8 - m if not want else m
    return msg, pltpu.roll(msg, by, 0)


def emit(nx, ny, v_ref, xp_ref, xm_ref, yp_ref, ym_ref):
    def one(x, y, m, want):
        return pack_faces(v_ref[x, y, 0:8], v_ref[x, y, 8:16], m, want)

    for y in range(ny):
        xp_ref[y] = one(0, y, 4, False)
        xm_ref[y] = one(nx - 1, y, 4, True)
    for x in range(nx):
        yp_ref[x] = one(x, 0, 2, False)
        ym_ref[x] = one(x, ny - 1, 2, True)


def prep_kernel(nx, ny, u_ref, v_ref, up_ref, *faces):
    def plane(x, _):
        for y in range(ny):
            rows = u_ref[pl.ds(x * ny + y, 16, stride=nx * ny), :]
            v_ref[x, y] = rows
            up_ref[x, y] = rows[8:]
        return 0

    lax.fori_loop(0, nx, plane, 0)
    emit(nx, ny, v_ref, *faces)


def pack_kernel(nx, ny, v_ref, uh_ref, ul_ref, zh_ref, zl_ref):
    def plane(x, _):
        odd = bit_of((16, 128), 0, 1)
        for y in range(ny):
            u = v_ref[x, y]
            uh_ref[x, y], ul_ref[x, y] = split2(u)
            mixed = jnp.where(odd, pltpu.roll(u, 1, 1), pltpu.roll(u, 127, 1))
            zh_ref[x, y], zl_ref[x, y] = split2(mixed)
        return 0

    lax.fori_loop(0, nx, plane, 0)


def table_kernel(nx, ny, vol_ref, face_ref, time_ref, slab_ref, r_ref, w_ref, rh_ref, rl_ref):
    classes = face_ref.shape[0]
    lane = lax.broadcasted_iota(jnp.int32, (16, 128), 1)
    row = lax.broadcasted_iota(jnp.int32, (16, 128), 0)
    eye = jnp.where(lane == row + 16, 1.0, 0.0)
    mats = [vol_ref[c] + eye for c in range(classes)]
    for k in range(16):
        for c in range(classes):
            a = mats[c]
            column = jnp.broadcast_to(a[:, k : k + 1], (16, 128))
            pivot = jnp.broadcast_to(column[k : k + 1], (16, 128))
            scaled = jnp.broadcast_to(a[k : k + 1], (16, 128)) / pivot
            factor = jnp.where(row == k, column - 1.0, column)
            mats[c] = a - factor * scaled
    alive = jnp.where(slab_ref[0] > 0, 1.0, 0.0)
    for c in range(classes):
        base = jnp.where(lane < 16, pltpu.roll(mats[c], 112, 1), 0.0) * DAMP
        total = base
        for place, m, minus, plus in ((16, 4, 0, 1), (32, 2, 2, 3), (48, 1, 4, 5)):
            high = (lane & m) != 0
            swapped = jnp.where(high, pltpu.roll(base, m, 1), pltpu.roll(base, 128 - m, 1))
            gain = jnp.where(high, face_ref[c, minus], face_ref[c, plus])
            block = jnp.where(lane < 16, swapped * gain, 0.0)
            total = total + pltpu.roll(block, place, 1)
        timed = jnp.where(lane < 8, base * (time_ref[c] * alive), 0.0)
        hi, lo = split2(total)
        thi, tlo = split2(timed)
        hi, lo, thi, tlo = (v.astype(F32) for v in (hi, lo, thi, tlo))
        rows = pl.ds(c * 16, 16)
        w_ref[rows, 0:128] = (hi + pltpu.roll(hi, 64, 1)).astype(BF16)
        second = lo + pltpu.roll(thi, 64, 1) + pltpu.roll(thi, 72, 1)
        second = second + pltpu.roll(tlo, 80, 1) + pltpu.roll(tlo, 88, 1)
        w_ref[rows, 128:256] = second.astype(BF16)

    def plane(x, _):
        for y in range(ny):
            r = r_ref[pl.ds(x * ny + y, 16, stride=nx * ny), :]
            rh_ref[x, y], rl_ref[x, y] = split2(r)
        return 0

    lax.fori_loop(0, nx, plane, 0)


def sweep_kernel(nx, ny, last, *refs):
    (w_ref, cls_ref, v_ref, rh_ref, rl_ref, uh_ref, ul_ref, zh_ref, zl_ref,
     before_ref, hxp_ref, hxm_ref, hyp_ref, hym_ref, *outs) = refs
    if last:
        out_ref, xph, xpl, xmh, xml, yph, ypl, ymh, yml = outs
    else:
        n_ref, up_ref, xp_ref, xm_ref, yp_ref, ym_ref, xph, xpl, xmh, xml, yph, ypl, ymh, yml = outs
    for src, hi_ref, lo_ref, m, want, count in (
        (hxp_ref, xph, xpl, 4, False, ny),
        (hxm_ref, xmh, xml, 4, True, ny),
        (hyp_ref, yph, ypl, 2, False, nx),
        (hym_ref, ymh, yml, 2, True, nx),
    ):
        for i in range(count):
            whole = jnp.concatenate(unpack_faces(src[i], m, want), axis=0)
            hi_ref[i], lo_ref[i] = split2(whole)
    xbit = bit_of((16, 128), 0, 4)
    ybit = bit_of((16, 128), 0, 2)

    def stack(x, y):
        tiles = []
        for uref, rref, zref, xp, xm, yp, ym in (
            (uh_ref, rh_ref, zh_ref, xph, xmh, yph, ymh),
            (ul_ref, rl_ref, zl_ref, xpl, xml, ypl, yml),
        ):
            ahead = jnp.where(x == nx - 1, xp[y], uref[jnp.minimum(x + 1, nx - 1), y])
            behind = jnp.where(x == 0, xm[y], uref[jnp.maximum(x - 1, 0), y])
            along_x = jnp.where(xbit, behind, ahead)
            right = yp[x] if y == ny - 1 else uref[x, y + 1]
            left = ym[x] if y == 0 else uref[x, y - 1]
            along_y = jnp.where(ybit, left, right)
            tiles.append([rref[x, y], along_x, along_y, zref[x, y]])
        b = before_ref[x, y]
        bh = b.astype(BF16).astype(F32)
        timed = jnp.concatenate([bh, b - bh], axis=0).astype(BF16)
        return jnp.concatenate(tiles[0] + tiles[1] + tiles[0] + [timed, timed], axis=0)

    def plane(x, _):
        for y in range(0, ny, 2):
            s = jnp.concatenate([stack(x, y), stack(x, y + 1)], axis=1)
            product = jnp.dot(w_ref[:, 0:224], s, preferred_element_type=F32)
            for k in range(2):
                cls = jnp.broadcast_to(cls_ref[x, y + k : y + k + 1, :], (8, 128))
                masks = [(cls & m) != 0 for m in (1, 2, 4)]
                halves = []
                for h in range(2):
                    level = [
                        product[c * 16 + h * 8 : c * 16 + h * 8 + 8, k * 128 : k * 128 + 128]
                        for c in range(8)
                    ]
                    for mask in masks:
                        level = [
                            jnp.where(mask, level[i + 1], level[i]) for i in range(0, len(level), 2)
                        ]
                    halves.append((1.0 - DAMP) * v_ref[x, y + k, h * 8 : h * 8 + 8] + level[0])
                whole = jnp.concatenate(halves, axis=0)
                if last:
                    out_ref[pl.ds(x * ny + y + k, 16, stride=nx * ny), :] = whole
                else:
                    n_ref[x, y + k] = whole
                    up_ref[x, y + k] = halves[1]
        return 0

    lax.fori_loop(0, nx, plane, 0)
    if not last:
        emit(nx, ny, n_ref, xp_ref, xm_ref, yp_ref, ym_ref)


def ring(axis, by):
    n = lax.axis_size(axis)
    return [(i, (i + by) % n) for i in range(n)]


def exchange(up, xp, xm, yp, ym):
    before = lax.ppermute(up, "tm", ring("tm", 1))
    hxp = lax.ppermute(xp, "sx", ring("sx", -1))
    hxm = lax.ppermute(xm, "sx", ring("sx", 1))
    hyp = lax.ppermute(yp, "sy", ring("sy", -1))
    hym = lax.ppermute(ym, "sy", ring("sy", 1))
    return before, hxp, hxm, hyp, hym


def call(kernel, ins, outs, name, scratch=(), flops=10**9, params=PARAMS):
    return pl.pallas_call(
        kernel,
        in_specs=ins,
        out_specs=[VMEM] * len(outs),
        out_shape=outs,
        scratch_shapes=scratch,
        compiler_params=params,
        cost_estimate=pl.CostEstimate(flops=flops, bytes_accessed=4 * 10**6, transcendentals=0),
        name=name,
    )


def on_device(right_side, current, classes, volume, face_gain, time_gain):
    _, nodes, nx, ny, nz = current.shape
    shape = jax.ShapeDtypeStruct
    faces = [shape((n, 8, nz), F32) for n in (ny, ny, nx, nx)]
    field = shape((nx, ny, nodes, nz), F32)
    half = shape((nx, ny, 8, nz), F32)
    packed = shape((nx, ny, nodes, nz), BF16)
    flat = (nodes * nx * ny, nz)
    u = current.reshape(flat)
    r = right_side.reshape(flat)
    cls = classes[0]
    slab = lax.axis_index("tm").reshape(1)
    vol = jnp.pad(volume, ((0, 0), (0, 0), (0, 112)))

    v, *sent = call(
        functools.partial(prep_kernel, nx, ny), [VMEM], [field, half] + faces, "prep"
    )(u)
    got = exchange(*sent)
    w, rh, rl = call(
        functools.partial(table_kernel, nx, ny),
        [VMEM, SMEM, SMEM, SMEM, VMEM],
        [shape((8 * nodes, 256), BF16), packed, packed],
        "tables",
    )(vol, face_gain, time_gain, slab, r)
    pack = call(functools.partial(pack_kernel, nx, ny), [VMEM], [packed] * 4, "pack")
    scratch = [pltpu.VMEM((n, 16, nz), BF16) for n in (ny, ny, ny, ny, nx, nx, nx, nx)]
    views = pack(v)
    v, *sent = call(
        functools.partial(sweep_kernel, nx, ny, False),
        [VMEM] * 14, [field, half] + faces, "sweep_a", scratch,
    )(w, cls, v, rh, rl, *views, *got)
    got = exchange(*sent)
    views = pack(v)
    (out,) = call(
        functools.partial(sweep_kernel, nx, ny, True),
        [VMEM] * 14, [shape(flat, F32)], "sweep_b", scratch,
    )(w, cls, v, rh, rl, *views, *got)
    return out.reshape(current.shape)


def solution(mesh):
    placed = (
        P("tm", None, "sx", "sy", None),
        P("tm", None, "sx", "sy", None),
        P("tm", "sx", "sy", None),
        P(),
        P(),
        P(),
    )
    return jax.shard_map(
        on_device,
        mesh=mesh,
        in_specs=placed,
        out_specs=P("tm", None, "sx", "sy", None),
        check_vma=False,
    )
```

```python
import functools
import jax
import jax.numpy as jnp
from jax import lax
from jax.experimental import pallas as pl
from jax.experimental.pallas import tpu as pltpu
from jax.sharding import PartitionSpec as P

F32 = jnp.float32
BF16 = jnp.bfloat16
DAMP = 0.7
GROUP = 4
VMEM = pl.BlockSpec(memory_space=pltpu.VMEM)
HBM = pl.BlockSpec(memory_space=pltpu.HBM)


def bit_of(shape, dim, m):
    return (lax.broadcasted_iota(jnp.int32, shape, dim) & m) != 0


def split2(v):
    hi = v.astype(BF16)
    lo = (v - hi.astype(F32)).astype(BF16)
    return hi, lo


def pack_faces(lower, upper, m, want):
    keep = bit_of(lower.shape, 0, m) == want
    by = m if not want else 8 - m
    return jnp.where(keep, lower, pltpu.roll(upper, by, 0))


def unpack_faces(msg, m, want):
    by = 8 - m if not want else m
    return msg, pltpu.roll(msg, by, 0)


def emit(nx, ny, place_ref, v_ref, xa_ref, xb_ref, ya_ref, yb_ref):
    def one(x, y, m, want):
        return pack_faces(v_ref[x, y, 0:8], v_ref[x, y, 8:16], m, want)

    def put(a_ref, b_ref, i, even, near, far):
        a_ref[i] = jnp.where(even, far, near)
        b_ref[i] = jnp.where(even, near, far)

    even_x = place_ref[1] == 0
    even_y = place_ref[2] == 0
    for y in range(ny):
        put(xa_ref, xb_ref, y, even_x, one(0, y, 4, False), one(nx - 1, y, 4, True))
    for x in range(nx):
        put(ya_ref, yb_ref, x, even_y, one(x, 0, 2, False), one(x, ny - 1, 2, True))


def prep_kernel(nx, ny, place_ref, u_ref, v_ref, up_ref, *rest):
    *faces, held_ref, sems = rest

    def copy(x):
        rows = pl.ds(x * ny, ny)
        return pltpu.make_async_copy(u_ref.at[:, rows], held_ref.at[:, rows], sems.at[x])

    for x in range(nx):
        copy(x).start()
    flat_ref = held_ref.reshape(16 * nx * ny, 128)

    for x in range(nx):
        copy(x).wait()
        for y in range(ny):
            rows = flat_ref[pl.ds(x * ny + y, 16, stride=nx * ny), :]
            v_ref[x, y] = rows
            up_ref[x, y] = rows[8:]
    emit(nx, ny, place_ref, v_ref, *faces)


def pack_kernel(nx, ny, v_ref, uh_ref, ul_ref, zh_ref, zl_ref):
    odd = bit_of((16, 128), 0, 1)
    for x in range(nx):
        for y in range(ny):
            u = v_ref[x, y]
            uh_ref[x, y], ul_ref[x, y] = split2(u)
            mixed = jnp.where(odd, pltpu.roll(u, 1, 1), pltpu.roll(u, 127, 1))
            zh_ref[x, y], zl_ref[x, y] = split2(mixed)


def inverses(vol_ref, wide_ref):
    lane = lax.broadcasted_iota(jnp.int32, (16, 128), 1)
    row = lax.broadcasted_iota(jnp.int32, (16, 128), 0)
    wide_ref[...] = jnp.zeros((128, 128), F32)
    wide_ref[:, 0:16] = vol_ref[...]
    turned = jnp.transpose(wide_ref[...])[0:16]
    mats = [turned if i == 0 else pltpu.roll(turned, 128 - i, 1) for i in range(16)]
    for k in range(16):
        scaled = jnp.where(row == k, 1.0, mats[k]) * (1.0 / mats[k][k : k + 1])
        for i in range(16):
            if i != k:
                factor = jnp.broadcast_to(mats[i][k : k + 1], (16, 128))
                mats[i] = jnp.where(row == k, 0.0, mats[i]) - factor * scaled
        mats[k] = scaled
    held = [jnp.where(lane % 16 == 0, m, 0.0) for m in mats]
    total = held[0]
    for i in range(1, 16):
        total = total + pltpu.roll(held[i], i, 1)
    return jnp.transpose(jnp.concatenate([total, jnp.zeros((112, 128), F32)], axis=0))


def table_kernel(nx, ny, place_ref, vol_ref, face_ref, time_ref, r_ref, w_ref, rh_ref, rl_ref, wide_ref):
    classes = face_ref.shape[0]
    lane = lax.broadcasted_iota(jnp.int32, (16, 128), 1)
    inverse = inverses(vol_ref, wide_ref)
    alive = jnp.where(place_ref[0, 0:1] > 0, 1.0, 0.0)
    spread = [jnp.broadcast_to(face_ref[:, k : k + 1], (classes, 128)) for k in range(6)]
    for c in range(classes):
        base = inverse[c * 16 : c * 16 + 16] * DAMP
        total = base
        for place, m, minus, plus in ((16, 4, 0, 1), (32, 2, 2, 3), (48, 1, 4, 5)):
            high = (lane & m) != 0
            swapped = jnp.where(high, pltpu.roll(base, m, 1), pltpu.roll(base, 128 - m, 1))
            gain = jnp.where(high, spread[minus][c : c + 1], spread[plus][c : c + 1])
            block = jnp.where(lane < 16, swapped * gain, 0.0)
            total = total + pltpu.roll(block, place, 1)
        gain = jnp.broadcast_to(time_ref[:, c : c + 1], (1, 128)) * alive
        timed = jnp.where(lane < 8, base * gain, 0.0)
        hi, lo = split2(total)
        thi, tlo = split2(timed)
        hi, lo, thi, tlo = (v.astype(F32) for v in (hi, lo, thi, tlo))
        rows = pl.ds(c * 16, 16)
        w_ref[rows, 0:128] = (hi + pltpu.roll(hi, 64, 1)).astype(BF16)
        second = lo + pltpu.roll(thi, 64, 1) + pltpu.roll(thi, 72, 1)
        second = second + pltpu.roll(tlo, 80, 1) + pltpu.roll(tlo, 88, 1)
        w_ref[rows, 128:256] = second.astype(BF16)

    for x in range(nx):
        for y in range(ny):
            r = r_ref[pl.ds(x * ny + y, 16, stride=nx * ny), :]
            rh_ref[x, y], rl_ref[x, y] = split2(r)


def sweep_kernel(nx, ny, last, *refs):
    (place_ref, w_ref, cls_ref, v_ref, rh_ref, rl_ref, uh_ref, ul_ref, zh_ref, zl_ref,
     before_ref, hxa_ref, hxb_ref, hyb_ref, hya_ref, *outs) = refs
    if last:
        out_ref, held_ref, sems, row_ref, xph, xpl, xmh, xml, yph, ypl, ymh, yml = outs
    else:
        n_ref, up_ref, xa_ref, xb_ref, ya_ref, yb_ref, xph, xpl, xmh, xml, yph, ypl, ymh, yml = outs
    even_x = place_ref[1] == 0
    even_y = place_ref[2] == 0
    for even, one_ref, two_ref, hi_ref, lo_ref, m, want, count in (
        (even_x, hxa_ref, hxb_ref, xph, xpl, 4, False, ny),
        (even_x, hxb_ref, hxa_ref, xmh, xml, 4, True, ny),
        (even_y, hya_ref, hyb_ref, yph, ypl, 2, False, nx),
        (even_y, hyb_ref, hya_ref, ymh, yml, 2, True, nx),
    ):
        for i in range(count):
            msg = jnp.where(even, one_ref[i], two_ref[i])
            whole = jnp.concatenate(unpack_faces(msg, m, want), axis=0)
            hi_ref[i], lo_ref[i] = split2(whole)
    xbit = bit_of((16, 128), 0, 4)
    ybit = bit_of((16, 128), 0, 2)

    def stack(x, y):
        tiles = []
        for uref, rref, zref, xp, xm, yp, ym in (
            (uh_ref, rh_ref, zh_ref, xph, xmh, yph, ymh),
            (ul_ref, rl_ref, zl_ref, xpl, xml, ypl, yml),
        ):
            ahead = xp[y] if x == nx - 1 else uref[x + 1, y]
            behind = xm[y] if x == 0 else uref[x - 1, y]
            along_x = jnp.where(xbit, behind, ahead)
            right = yp[x] if y == ny - 1 else uref[x, y + 1]
            left = ym[x] if y == 0 else uref[x, y - 1]
            along_y = jnp.where(ybit, left, right)
            tiles.append([rref[x, y], along_x, along_y, zref[x, y]])
        b = before_ref[x, y]
        bh = b.astype(BF16).astype(F32)
        timed = jnp.concatenate([bh, b - bh], axis=0).astype(BF16)
        return jnp.concatenate(tiles[0] + tiles[1] + tiles[0] + [timed, timed], axis=0)

    def copy(x):
        rows = pl.ds(x * ny, ny)
        return pltpu.make_async_copy(held_ref.at[:, rows], out_ref.at[:, rows], sems.at[x])

    def turn(x):
        for node in range(16):
            for y in range(0, ny, 8):
                rows = row_ref[pl.ds((x * ny + y) * 16 + node, 8, stride=16), :]
                held_ref[node, x * ny + y : x * ny + y + 8, :] = rows

    def plane(x):
        for y in range(0, ny, 2):
            s = jnp.concatenate([stack(x, y), stack(x, y + 1)], axis=1)
            product = jnp.dot(w_ref[:, 0:224], s, preferred_element_type=F32)
            for k in range(2):
                cls = jnp.broadcast_to(cls_ref[x, y + k : y + k + 1, :], (8, 128))
                masks = [(cls & m) != 0 for m in (1, 2, 4)]
                halves = []
                for h in range(2):
                    level = [
                        product[c * 16 + h * 8 : c * 16 + h * 8 + 8, k * 128 : k * 128 + 128]
                        for c in range(8)
                    ]
                    for mask in masks:
                        level = [
                            jnp.where(mask, level[i + 1], level[i]) for i in range(0, len(level), 2)
                        ]
                    halves.append((1.0 - DAMP) * v_ref[x, y + k, h * 8 : h * 8 + 8] + level[0])
                whole = jnp.concatenate(halves, axis=0)
                if last:
                    row_ref[pl.ds((x * ny + y + k) * 16, 16), :] = whole
                else:
                    n_ref[x, y + k] = whole
                    up_ref[x, y + k] = halves[1]
        if last:
            turn(x)
            if x % GROUP == GROUP - 1:
                for z in range(x - GROUP + 1, x + 1):
                    copy(z).start()

    for x in range(nx):
        plane(x)
    if last:
        for x in range(nx):
            copy(x).wait()
    else:
        emit(nx, ny, place_ref, n_ref, xa_ref, xb_ref, ya_ref, yb_ref)


def ring(axis, by):
    n = lax.axis_size(axis)
    return [(i, (i + by) % n) for i in range(n)]


def pairs(axis):
    n = lax.axis_size(axis)
    first = [(i, i ^ 1) for i in range(n)]
    second = [(i, (i + 1 if i % 2 else i - 1) % n) for i in range(n)]
    return first, second


def exchange(up, xa, xb, ya, yb):
    before = lax.ppermute(up, "tm", ring("tm", 1))
    (x_one, x_two), (y_one, y_two) = pairs("sx"), pairs("sy")
    return (
        before,
        lax.ppermute(xa, "sx", x_one),
        lax.ppermute(xb, "sx", x_two),
        lax.ppermute(yb, "sy", y_two),
        lax.ppermute(ya, "sy", y_one),
    )


def call(kernel, ins, outs, name, scratch=(), flops=10**9, grant=40):
    return pl.pallas_call(
        kernel,
        in_specs=ins,
        out_specs=[VMEM] * len(outs) if len(outs) > 1 else [HBM],
        out_shape=outs,
        scratch_shapes=scratch,
        compiler_params=pltpu.CompilerParams(vmem_limit_bytes=grant * 1024 * 1024),
        cost_estimate=pl.CostEstimate(flops=flops, bytes_accessed=4 * 10**6, transcendentals=0),
        name=name,
    )


def on_device(right_side, current, classes, volume, face_gain, time_gain):
    _, nodes, nx, ny, nz = current.shape
    shape = jax.ShapeDtypeStruct
    faces = [shape((n, 8, nz), F32) for n in (ny, ny, nx, nx)]
    field = shape((nx, ny, nodes, nz), F32)
    half = shape((nx, ny, 8, nz), F32)
    packed = shape((nx, ny, nodes, nz), BF16)
    cube = (nodes, nx * ny, nz)
    r = right_side.reshape(nodes * nx * ny, nz)
    stream = [pltpu.VMEM(cube, F32), pltpu.SemaphoreType.DMA((nx,))]
    cls = classes[0]
    place = jnp.stack([lax.axis_index("tm"), lax.axis_index("sx") % 2, lax.axis_index("sy") % 2])
    place = jnp.broadcast_to(place[:, None, None], (3, 8, nz))
    vol = volume.reshape(volume.shape[0] * nodes, nodes)

    v, *sent = call(
        functools.partial(prep_kernel, nx, ny), [VMEM, HBM], [field, half] + faces, "prep", stream, grant=52
    )(place, current.reshape(cube))
    got = exchange(*sent)
    w, rh, rl = call(
        functools.partial(table_kernel, nx, ny),
        [VMEM] * 5,
        [shape((8 * nodes, 256), BF16), packed, packed],
        "tables", [pltpu.VMEM((128, 128), F32)],
    )(place, vol, face_gain, time_gain.reshape(1, -1), r)
    pack = call(functools.partial(pack_kernel, nx, ny), [VMEM], [packed] * 4, "pack")
    scratch = [pltpu.VMEM((n, 16, nz), BF16) for n in (ny, ny, ny, ny, nx, nx, nx, nx)]
    views = pack(v)
    v, *sent = call(
        functools.partial(sweep_kernel, nx, ny, False),
        [VMEM] * 15, [field, half] + faces, "sweep_a", scratch,
    )(place, w, cls, v, rh, rl, *views, *got)
    got = exchange(*sent)
    views = pack(v)
    (out,) = call(
        functools.partial(sweep_kernel, nx, ny, True),
        [VMEM] * 15, [shape(cube, F32)], "sweep_b", stream + [pltpu.VMEM((nx * ny * nodes, nz), F32)] + scratch,
    )(place, w, cls, v, rh, rl, *views, *got)
    return out.reshape(current.shape)


def solution(mesh):
    placed = (
        P("tm", None, "sx", "sy", None),
        P("tm", None, "sx", "sy", None),
        P("tm", "sx", "sy", None),
        P(),
        P(),
        P(),
    )
    return jax.shard_map(
        on_device,
        mesh=mesh,
        in_specs=placed,
        out_specs=P("tm", None, "sx", "sy", None),
        check_vma=False,
    )
```

```python
import functools
import jax
import jax.numpy as jnp
from jax import lax
from jax.experimental import pallas as pl
from jax.experimental.pallas import tpu as pltpu
from jax.sharding import PartitionSpec as P

F32 = jnp.float32
BF16 = jnp.bfloat16
DAMP = 0.7
VMEM = pl.BlockSpec(memory_space=pltpu.VMEM)
HBM = pl.BlockSpec(memory_space=pltpu.HBM)


def bit_of(shape, dim, m):
    return (lax.broadcasted_iota(jnp.int32, shape, dim) & m) != 0


def split2(v):
    hi = v.astype(BF16)
    lo = (v - hi.astype(F32)).astype(BF16)
    return hi, lo


def pack_faces(lower, upper, m, want):
    keep = bit_of(lower.shape, 0, m) == want
    by = m if not want else 8 - m
    return jnp.where(keep, lower, pltpu.roll(upper, by, 0))


def unpack_faces(msg, m, want):
    by = 8 - m if not want else m
    return msg, pltpu.roll(msg, by, 0)


def emit(nx, ny, place_ref, v_ref, xa_ref, xb_ref, ya_ref, yb_ref):
    def one(x, y, m, want):
        return pack_faces(v_ref[x, y, 0:8], v_ref[x, y, 8:16], m, want)

    def put(a_ref, b_ref, i, even, near, far):
        a_ref[i] = jnp.where(even, far, near)
        b_ref[i] = jnp.where(even, near, far)

    even_x = place_ref[1] == 0
    even_y = place_ref[2] == 0
    for y in range(ny):
        put(xa_ref, xb_ref, y, even_x, one(0, y, 4, False), one(nx - 1, y, 4, True))
    for x in range(nx):
        put(ya_ref, yb_ref, x, even_y, one(x, 0, 2, False), one(x, ny - 1, 2, True))


def prep_kernel(nx, ny, place_ref, u_ref, v_ref, up_ref, *rest):
    *faces, held_ref, sems = rest

    def copy(x):
        rows = pl.ds(x * ny, ny)
        return pltpu.make_async_copy(u_ref.at[:, rows], held_ref.at[:, rows], sems.at[x])

    for x in range(nx):
        copy(x).start()
    flat_ref = held_ref.reshape(16 * nx * ny, 128)

    for x in range(nx):
        copy(x).wait()
        for y in range(ny):
            rows = flat_ref[pl.ds(x * ny + y, 16, stride=nx * ny), :]
            v_ref[x, y] = rows
            up_ref[x, y] = rows[8:]
    emit(nx, ny, place_ref, v_ref, *faces)


def pack_kernel(nx, ny, v_ref, uh_ref, ul_ref, zh_ref, zl_ref):
    odd = bit_of((16, 128), 0, 1)
    for x in range(nx):
        for y in range(ny):
            u = v_ref[x, y]
            uh_ref[x, y], ul_ref[x, y] = split2(u)
            mixed = jnp.where(odd, pltpu.roll(u, 1, 1), pltpu.roll(u, 127, 1))
            zh_ref[x, y], zl_ref[x, y] = split2(mixed)


def both_kernel(nx, ny, v_ref, r_ref, uh_ref, ul_ref, zh_ref, zl_ref, rh_ref, rl_ref):
    pack_kernel(nx, ny, v_ref, uh_ref, ul_ref, zh_ref, zl_ref)
    for x in range(nx):
        for y in range(ny):
            r = r_ref[pl.ds(x * ny + y, 16, stride=nx * ny), :]
            rh_ref[x, y], rl_ref[x, y] = split2(r)


def inverses(vol_ref, wide_ref):
    lane = lax.broadcasted_iota(jnp.int32, (16, 128), 1)
    row = lax.broadcasted_iota(jnp.int32, (16, 128), 0)
    wide_ref[...] = jnp.zeros((128, 128), F32)
    wide_ref[:, 0:16] = vol_ref[...]
    turned = jnp.transpose(wide_ref[...])[0:16]
    mats = [turned if i == 0 else pltpu.roll(turned, 128 - i, 1) for i in range(16)]
    for k in range(16):
        scaled = jnp.where(row == k, 1.0, mats[k]) * (1.0 / mats[k][k : k + 1])
        for i in range(16):
            if i != k:
                factor = jnp.broadcast_to(mats[i][k : k + 1], (16, 128))
                mats[i] = jnp.where(row == k, 0.0, mats[i]) - factor * scaled
        mats[k] = scaled
    held = [jnp.where(lane % 16 == 0, m, 0.0) for m in mats]
    total = held[0]
    for i in range(1, 16):
        total = total + pltpu.roll(held[i], i, 1)
    return jnp.transpose(jnp.concatenate([total, jnp.zeros((112, 128), F32)], axis=0))


def table_kernel(place_ref, vol_ref, face_ref, time_ref, w_ref, wide_ref):
    classes = face_ref.shape[0]
    lane = lax.broadcasted_iota(jnp.int32, (16, 128), 1)
    inverse = inverses(vol_ref, wide_ref)
    alive = jnp.where(place_ref[0, 0:1] > 0, 1.0, 0.0)
    spread = [jnp.broadcast_to(face_ref[:, k : k + 1], (classes, 128)) for k in range(6)]
    for c in range(classes):
        base = inverse[c * 16 : c * 16 + 16] * DAMP
        total = base
        for place, m, minus, plus in ((16, 4, 0, 1), (32, 2, 2, 3), (48, 1, 4, 5)):
            high = (lane & m) != 0
            swapped = jnp.where(high, pltpu.roll(base, m, 1), pltpu.roll(base, 128 - m, 1))
            gain = jnp.where(high, spread[minus][c : c + 1], spread[plus][c : c + 1])
            block = jnp.where(lane < 16, swapped * gain, 0.0)
            total = total + pltpu.roll(block, place, 1)
        gain = jnp.broadcast_to(time_ref[:, c : c + 1], (1, 128)) * alive
        timed = jnp.where(lane < 8, base * gain, 0.0)
        hi, lo = split2(total)
        thi, tlo = split2(timed)
        hi, lo, thi, tlo = (v.astype(F32) for v in (hi, lo, thi, tlo))
        rows = pl.ds(c * 16, 16)
        w_ref[rows, 0:128] = (hi + pltpu.roll(hi, 64, 1)).astype(BF16)
        second = lo + pltpu.roll(thi, 64, 1) + pltpu.roll(thi, 72, 1)
        second = second + pltpu.roll(tlo, 80, 1) + pltpu.roll(tlo, 88, 1)
        w_ref[rows, 128:256] = second.astype(BF16)


def sweep_kernel(nx, ny, last, *refs):
    (place_ref, w_ref, cls_ref, v_ref, rh_ref, rl_ref, uh_ref, ul_ref, zh_ref, zl_ref,
     before_ref, hxa_ref, hxb_ref, hyb_ref, hya_ref, *outs) = refs
    if last:
        out_ref, held_ref, sems, row_ref, xph, xpl, xmh, xml, yph, ypl, ymh, yml = outs
    else:
        n_ref, up_ref, xa_ref, xb_ref, ya_ref, yb_ref, xph, xpl, xmh, xml, yph, ypl, ymh, yml = outs
    even_x = place_ref[1] == 0
    even_y = place_ref[2] == 0
    for even, one_ref, two_ref, hi_ref, lo_ref, m, want, count in (
        (even_x, hxa_ref, hxb_ref, xph, xpl, 4, False, ny),
        (even_x, hxb_ref, hxa_ref, xmh, xml, 4, True, ny),
        (even_y, hya_ref, hyb_ref, yph, ypl, 2, False, nx),
        (even_y, hyb_ref, hya_ref, ymh, yml, 2, True, nx),
    ):
        for i in range(count):
            msg = jnp.where(even, one_ref[i], two_ref[i])
            whole = jnp.concatenate(unpack_faces(msg, m, want), axis=0)
            hi_ref[i], lo_ref[i] = split2(whole)
    xbit = bit_of((16, 128), 0, 4)
    ybit = bit_of((16, 128), 0, 2)

    def stack(x, y):
        tiles = []
        for uref, rref, zref, xp, xm, yp, ym in (
            (uh_ref, rh_ref, zh_ref, xph, xmh, yph, ymh),
            (ul_ref, rl_ref, zl_ref, xpl, xml, ypl, yml),
        ):
            ahead = xp[y] if x == nx - 1 else uref[x + 1, y]
            behind = xm[y] if x == 0 else uref[x - 1, y]
            along_x = jnp.where(xbit, behind, ahead)
            right = yp[x] if y == ny - 1 else uref[x, y + 1]
            left = ym[x] if y == 0 else uref[x, y - 1]
            along_y = jnp.where(ybit, left, right)
            tiles.append([rref[x, y], along_x, along_y, zref[x, y]])
        b = before_ref[x, y]
        bh = b.astype(BF16).astype(F32)
        timed = jnp.concatenate([bh, b - bh], axis=0).astype(BF16)
        return jnp.concatenate(tiles[0] + tiles[1] + tiles[0] + [timed, timed], axis=0)

    def copy(x):
        rows = pl.ds(x * ny, ny)
        return pltpu.make_async_copy(held_ref.at[:, rows], out_ref.at[:, rows], sems.at[x])

    def turn(x):
        for node in range(16):
            for y in range(0, ny, 8):
                rows = row_ref[pl.ds((x * ny + y) * 16 + node, 8, stride=16), :]
                held_ref[node, x * ny + y : x * ny + y + 8, :] = rows

    def plane(x):
        for y in range(0, ny, 2):
            s = jnp.concatenate([stack(x, y), stack(x, y + 1)], axis=1)
            product = jnp.dot(w_ref[:, 0:224], s, preferred_element_type=F32)
            for k in range(2):
                cls = jnp.broadcast_to(cls_ref[x, y + k : y + k + 1, :], (8, 128))
                masks = [(cls & m) != 0 for m in (1, 2, 4)]
                halves = []
                for h in range(2):
                    level = [
                        product[c * 16 + h * 8 : c * 16 + h * 8 + 8, k * 128 : k * 128 + 128]
                        for c in range(8)
                    ]
                    for mask in masks:
                        level = [
                            jnp.where(mask, level[i + 1], level[i]) for i in range(0, len(level), 2)
                        ]
                    halves.append((1.0 - DAMP) * v_ref[x, y + k, h * 8 : h * 8 + 8] + level[0])
                whole = jnp.concatenate(halves, axis=0)
                if last:
                    row_ref[pl.ds((x * ny + y + k) * 16, 16), :] = whole
                else:
                    n_ref[x, y + k] = whole
                    up_ref[x, y + k] = halves[1]
        if last:
            turn(x)
            if x in (nx // 2, nx - 1):
                for z in range(nx // 2 + 1) if x == nx // 2 else range(nx // 2 + 1, nx):
                    copy(z).start()

    for x in range(nx):
        plane(x)
    if last:
        for x in range(nx):
            copy(x).wait()
    else:
        emit(nx, ny, place_ref, n_ref, xa_ref, xb_ref, ya_ref, yb_ref)


def ring(axis, by):
    n = lax.axis_size(axis)
    return [(i, (i + by) % n) for i in range(n)]


def pairs(axis):
    n = lax.axis_size(axis)
    first = [(i, i ^ 1) for i in range(n)]
    second = [(i, (i + 1 if i % 2 else i - 1) % n) for i in range(n)]
    return first, second


def exchange(up, xa, xb, ya, yb):
    before = lax.ppermute(up, "tm", ring("tm", 1))
    (x_one, x_two), (y_one, y_two) = pairs("sx"), pairs("sy")
    return (
        before,
        lax.ppermute(xa, "sx", x_one),
        lax.ppermute(xb, "sx", x_two),
        lax.ppermute(yb, "sy", y_two),
        lax.ppermute(ya, "sy", y_one),
    )


def call(kernel, ins, outs, name, scratch=(), flops=10**9, grant=40, streamed=False):
    return pl.pallas_call(
        kernel,
        in_specs=ins,
        out_specs=[HBM if streamed else VMEM] * len(outs),
        out_shape=outs,
        scratch_shapes=scratch,
        compiler_params=pltpu.CompilerParams(vmem_limit_bytes=grant * 1024 * 1024),
        cost_estimate=pl.CostEstimate(flops=flops, bytes_accessed=4 * 10**6, transcendentals=0),
        name=name,
    )


def on_device(right_side, current, classes, volume, face_gain, time_gain):
    _, nodes, nx, ny, nz = current.shape
    shape = jax.ShapeDtypeStruct
    faces = [shape((n, 8, nz), F32) for n in (ny, ny, nx, nx)]
    field = shape((nx, ny, nodes, nz), F32)
    half = shape((nx, ny, 8, nz), F32)
    packed = shape((nx, ny, nodes, nz), BF16)
    cube = (nodes, nx * ny, nz)
    r = right_side.reshape(nodes * nx * ny, nz)
    stream = [pltpu.VMEM(cube, F32), pltpu.SemaphoreType.DMA((nx,))]
    cls = classes[0]
    which = lax.broadcasted_iota(jnp.int32, (3, 8, nz), 0)
    odd_x, odd_y = lax.axis_index("sx") % 2, lax.axis_index("sy") % 2
    place = jnp.where(which == 0, lax.axis_index("tm"), jnp.where(which == 1, odd_x, odd_y))
    vol = volume.reshape(volume.shape[0] * nodes, nodes)

    v, *sent = call(
        functools.partial(prep_kernel, nx, ny), [VMEM, HBM], [field, half] + faces, "prep", stream, grant=52
    )(place, current.reshape(cube))
    got = exchange(*sent)
    (w,) = call(
        table_kernel, [VMEM] * 4, [shape((8 * nodes, 256), BF16)], "tables", [pltpu.VMEM((128, 128), F32)]
    )(place, vol, face_gain, time_gain.reshape(1, -1))
    *views, rh, rl = call(
        functools.partial(both_kernel, nx, ny), [VMEM] * 2, [packed] * 6, "both"
    )(v, r)
    pack = call(functools.partial(pack_kernel, nx, ny), [VMEM], [packed] * 4, "pack")
    scratch = [pltpu.VMEM((n, 16, nz), BF16) for n in (ny, ny, ny, ny, nx, nx, nx, nx)]
    v, *sent = call(
        functools.partial(sweep_kernel, nx, ny, False),
        [VMEM] * 15, [field, half] + faces, "sweep_a", scratch,
    )(place, w, cls, v, rh, rl, *views, *got)
    got = exchange(*sent)
    views = pack(v)
    (out,) = call(
        functools.partial(sweep_kernel, nx, ny, True),
        [VMEM] * 15, [shape(cube, F32)], "sweep_b", stream + [pltpu.VMEM((nx * ny * nodes, nz), F32)] + scratch, streamed=True,
    )(place, w, cls, v, rh, rl, *views, *got)
    return out.reshape(current.shape)


def solution(mesh):
    placed = (
        P("tm", None, "sx", "sy", None),
        P("tm", None, "sx", "sy", None),
        P("tm", "sx", "sy", None),
        P(),
        P(),
        P(),
    )
    return jax.shard_map(
        on_device,
        mesh=mesh,
        in_specs=placed,
        out_specs=P("tm", None, "sx", "sy", None),
        check_vma=False,
    )
```

```python
import functools
import jax
import jax.numpy as jnp
from jax import lax
from jax.experimental import pallas as pl
from jax.experimental.pallas import tpu as pltpu
from jax.sharding import PartitionSpec as P

F32 = jnp.float32
BF16 = jnp.bfloat16
DAMP = 0.7
VMEM = pl.BlockSpec(memory_space=pltpu.VMEM)
HBM = pl.BlockSpec(memory_space=pltpu.HBM)


def bit_of(shape, dim, m):
    return (lax.broadcasted_iota(jnp.int32, shape, dim) & m) != 0


def split2(v):
    hi = v.astype(BF16)
    lo = (v - hi.astype(F32)).astype(BF16)
    return hi, lo


def pack_faces(lower, upper, m, want):
    keep = bit_of(lower.shape, 0, m) == want
    by = m if not want else 8 - m
    return jnp.where(keep, lower, pltpu.roll(upper, by, 0))


def unpack_faces(msg, m, want):
    by = 8 - m if not want else m
    return msg, pltpu.roll(msg, by, 0)


def emit(nx, ny, place_ref, v_ref, xa_ref, xb_ref, ya_ref, yb_ref):
    def one(x, y, m, want):
        return pack_faces(v_ref[x, y, 0:8], v_ref[x, y, 8:16], m, want)

    def put(a_ref, b_ref, i, even, near, far):
        a_ref[i] = jnp.where(even, far, near)
        b_ref[i] = jnp.where(even, near, far)

    even_x = place_ref[1] == 0
    even_y = place_ref[2] == 0
    for y in range(ny):
        put(xa_ref, xb_ref, y, even_x, one(0, y, 4, False), one(nx - 1, y, 4, True))
    for x in range(nx):
        put(ya_ref, yb_ref, x, even_y, one(x, 0, 2, False), one(x, ny - 1, 2, True))


def prep_kernel(nx, ny, place_ref, u_ref, v_ref, up_ref, *rest):
    *faces, held_ref, sems = rest

    def copy(x):
        rows = pl.ds(x * ny, ny)
        return pltpu.make_async_copy(u_ref.at[:, rows], held_ref.at[:, rows], sems.at[x])

    for x in range(nx):
        copy(x).start()
    flat_ref = held_ref.reshape(16 * nx * ny, 128)

    for x in range(nx):
        copy(x).wait()
        for y in range(ny):
            rows = flat_ref[pl.ds(x * ny + y, 16, stride=nx * ny), :]
            v_ref[x, y] = rows
            up_ref[x, y] = rows[8:]
    emit(nx, ny, place_ref, v_ref, *faces)


def pack_kernel(nx, ny, v_ref, uh_ref, ul_ref, zh_ref, zl_ref):
    odd = bit_of((16, 128), 0, 1)
    for x in range(nx):
        for y in range(ny):
            u = v_ref[x, y]
            uh_ref[x, y], ul_ref[x, y] = split2(u)
            mixed = jnp.where(odd, pltpu.roll(u, 1, 1), pltpu.roll(u, 127, 1))
            zh_ref[x, y], zl_ref[x, y] = split2(mixed)


def both_kernel(nx, ny, v_ref, r_ref, time_ref, uh_ref, ul_ref, zh_ref, zl_ref, rh_ref, rl_ref):
    pack_kernel(nx, ny, v_ref, uh_ref, ul_ref, zh_ref, zl_ref)
    for x in range(nx):
        for y in range(ny):
            r = r_ref[pl.ds(x * ny + y, 16, stride=nx * ny), :]
            rh_ref[x, y], rl_ref[x, y] = split2(r)


def inverses(vol_ref, wide_ref):
    lane = lax.broadcasted_iota(jnp.int32, (16, 128), 1)
    row = lax.broadcasted_iota(jnp.int32, (16, 128), 0)
    wide_ref[...] = jnp.zeros((128, 128), F32)
    wide_ref[:, 0:16] = vol_ref[...]
    turned = jnp.transpose(wide_ref[...])[0:16]
    mats = [turned if i == 0 else pltpu.roll(turned, 128 - i, 1) for i in range(16)]
    for k in range(16):
        scaled = jnp.where(row == k, 1.0, mats[k]) * (1.0 / mats[k][k : k + 1])
        for i in range(16):
            if i != k:
                factor = jnp.broadcast_to(mats[i][k : k + 1], (16, 128))
                mats[i] = jnp.where(row == k, 0.0, mats[i]) - factor * scaled
        mats[k] = scaled
    held = [jnp.where(lane % 16 == 0, m, 0.0) for m in mats]
    total = held[0]
    for i in range(1, 16):
        total = total + pltpu.roll(held[i], i, 1)
    return jnp.transpose(jnp.concatenate([total, jnp.zeros((112, 128), F32)], axis=0))


def table_kernel(place_ref, vol_ref, face_ref, time_ref, w_ref, wide_ref):
    classes = face_ref.shape[0]
    lane = lax.broadcasted_iota(jnp.int32, (16, 128), 1)
    inverse = inverses(vol_ref, wide_ref)
    alive = jnp.where(place_ref[0, 0:1] > 0, 1.0, 0.0)
    spread = [jnp.broadcast_to(face_ref[:, k : k + 1], (classes, 128)) for k in range(6)]
    for c in range(classes):
        base = inverse[c * 16 : c * 16 + 16] * DAMP
        total = base
        for place, m, minus, plus in ((16, 4, 0, 1), (32, 2, 2, 3), (48, 1, 4, 5)):
            high = (lane & m) != 0
            swapped = jnp.where(high, pltpu.roll(base, m, 1), pltpu.roll(base, 128 - m, 1))
            gain = jnp.where(high, spread[minus][c : c + 1], spread[plus][c : c + 1])
            block = jnp.where(lane < 16, swapped * gain, 0.0)
            total = total + pltpu.roll(block, place, 1)
        gain = jnp.broadcast_to(time_ref[:, c : c + 1], (1, 128)) * alive
        timed = jnp.where(lane < 8, base * gain, 0.0)
        hi, lo = split2(total)
        thi, tlo = split2(timed)
        hi, lo, thi, tlo = (v.astype(F32) for v in (hi, lo, thi, tlo))
        rows = pl.ds(c * 16, 16)
        w_ref[rows, 0:128] = (hi + pltpu.roll(hi, 64, 1)).astype(BF16)
        second = lo + pltpu.roll(thi, 64, 1) + pltpu.roll(thi, 72, 1)
        second = second + pltpu.roll(tlo, 80, 1) + pltpu.roll(tlo, 88, 1)
        w_ref[rows, 128:256] = second.astype(BF16)


def sweep_kernel(nx, ny, last, *refs):
    (place_ref, w_ref, cls_ref, v_ref, rh_ref, rl_ref, uh_ref, ul_ref, zh_ref, zl_ref,
     before_ref, hxa_ref, hxb_ref, hyb_ref, hya_ref, *outs) = refs
    if last:
        out_ref, held_ref, sems, row_ref, xph, xpl, xmh, xml, yph, ypl, ymh, yml = outs
    else:
        n_ref, up_ref, xa_ref, xb_ref, ya_ref, yb_ref, xph, xpl, xmh, xml, yph, ypl, ymh, yml = outs
    even_x = place_ref[1] == 0
    even_y = place_ref[2] == 0
    for even, one_ref, two_ref, hi_ref, lo_ref, m, want, count in (
        (even_x, hxa_ref, hxb_ref, xph, xpl, 4, False, ny),
        (even_x, hxb_ref, hxa_ref, xmh, xml, 4, True, ny),
        (even_y, hya_ref, hyb_ref, yph, ypl, 2, False, nx),
        (even_y, hyb_ref, hya_ref, ymh, yml, 2, True, nx),
    ):
        for i in range(count):
            msg = jnp.where(even, one_ref[i], two_ref[i])
            whole = jnp.concatenate(unpack_faces(msg, m, want), axis=0)
            hi_ref[i], lo_ref[i] = split2(whole)
    xbit = bit_of((16, 128), 0, 4)
    ybit = bit_of((16, 128), 0, 2)

    def stack(x, y):
        tiles = []
        for uref, rref, zref, xp, xm, yp, ym in (
            (uh_ref, rh_ref, zh_ref, xph, xmh, yph, ymh),
            (ul_ref, rl_ref, zl_ref, xpl, xml, ypl, yml),
        ):
            ahead = xp[y] if x == nx - 1 else uref[x + 1, y]
            behind = xm[y] if x == 0 else uref[x - 1, y]
            along_x = jnp.where(xbit, behind, ahead)
            right = yp[x] if y == ny - 1 else uref[x, y + 1]
            left = ym[x] if y == 0 else uref[x, y - 1]
            along_y = jnp.where(ybit, left, right)
            tiles.append([rref[x, y], along_x, along_y, zref[x, y]])
        b = before_ref[x, y]
        bh = b.astype(BF16).astype(F32)
        timed = jnp.concatenate([bh, b - bh], axis=0).astype(BF16)
        return jnp.concatenate(tiles[0] + tiles[1] + tiles[0] + [timed, timed], axis=0)

    def copy(x):
        rows = pl.ds(x * ny, ny)
        return pltpu.make_async_copy(held_ref.at[:, rows], out_ref.at[:, rows], sems.at[x])

    def turn(x):
        for node in range(16):
            for y in range(0, ny, 8):
                rows = row_ref[pl.ds((x * ny + y) * 16 + node, 8, stride=16), :]
                held_ref[node, x * ny + y : x * ny + y + 8, :] = rows

    def plane(x):
        for y in range(0, ny, 2):
            s = jnp.concatenate([stack(x, y), stack(x, y + 1)], axis=1)
            product = jnp.dot(w_ref[:, 0:224], s, preferred_element_type=F32)
            for k in range(2):
                cls = jnp.broadcast_to(cls_ref[x, y + k : y + k + 1, :], (8, 128))
                masks = [(cls & m) != 0 for m in (1, 2, 4)]
                halves = []
                for h in range(2):
                    level = [
                        product[c * 16 + h * 8 : c * 16 + h * 8 + 8, k * 128 : k * 128 + 128]
                        for c in range(8)
                    ]
                    for mask in masks:
                        level = [
                            jnp.where(mask, level[i + 1], level[i]) for i in range(0, len(level), 2)
                        ]
                    halves.append((1.0 - DAMP) * v_ref[x, y + k, h * 8 : h * 8 + 8] + level[0])
                whole = jnp.concatenate(halves, axis=0)
                if last:
                    row_ref[pl.ds((x * ny + y + k) * 16, 16), :] = whole
                else:
                    n_ref[x, y + k] = whole
                    up_ref[x, y + k] = halves[1]
        if last:
            turn(x)
            if x in (nx // 2, nx - 1):
                for z in range(nx // 2 + 1) if x == nx // 2 else range(nx // 2 + 1, nx):
                    copy(z).start()

    for x in range(nx):
        plane(x)
    if last:
        for x in range(nx):
            copy(x).wait()
    else:
        emit(nx, ny, place_ref, n_ref, xa_ref, xb_ref, ya_ref, yb_ref)


def ring(axis, by):
    n = lax.axis_size(axis)
    return [(i, (i + by) % n) for i in range(n)]


def pairs(axis):
    n = lax.axis_size(axis)
    first = [(i, i ^ 1) for i in range(n)]
    second = [(i, (i + 1 if i % 2 else i - 1) % n) for i in range(n)]
    return first, second


def exchange(up, xa, xb, ya, yb):
    before = lax.ppermute(up, "tm", ring("tm", 1))
    (x_one, x_two), (y_one, y_two) = pairs("sx"), pairs("sy")
    return (
        before,
        lax.ppermute(xa, "sx", x_one),
        lax.ppermute(xb, "sx", x_two),
        lax.ppermute(yb, "sy", y_two),
        lax.ppermute(ya, "sy", y_one),
    )


def call(kernel, ins, outs, name, scratch=(), flops=10**9, grant=40, streamed=False):
    return pl.pallas_call(
        kernel,
        in_specs=ins,
        out_specs=[HBM if streamed else VMEM] * len(outs),
        out_shape=outs,
        scratch_shapes=scratch,
        compiler_params=pltpu.CompilerParams(vmem_limit_bytes=grant * 1024 * 1024),
        cost_estimate=pl.CostEstimate(flops=flops, bytes_accessed=4 * 10**6, transcendentals=0),
        name=name,
    )


def on_device(right_side, current, classes, volume, face_gain, time_gain):
    _, nodes, nx, ny, nz = current.shape
    shape = jax.ShapeDtypeStruct
    faces = [shape((n, 8, nz), F32) for n in (ny, ny, nx, nx)]
    field = shape((nx, ny, nodes, nz), F32)
    half = shape((nx, ny, 8, nz), F32)
    packed = shape((nx, ny, nodes, nz), BF16)
    cube = (nodes, nx * ny, nz)
    r = right_side.reshape(nodes * nx * ny, nz)
    stream = [pltpu.VMEM(cube, F32), pltpu.SemaphoreType.DMA((nx,))]
    cls = classes[0]
    which = lax.broadcasted_iota(jnp.int32, (3, 8, nz), 0)
    odd_x, odd_y = lax.axis_index("sx") % 2, lax.axis_index("sy") % 2
    place = jnp.where(which == 0, lax.axis_index("tm"), jnp.where(which == 1, odd_x, odd_y))
    vol = volume.reshape(volume.shape[0] * nodes, nodes)
    small = (vol, face_gain, time_gain.reshape(1, -1))

    v, *sent = call(
        functools.partial(prep_kernel, nx, ny), [VMEM, HBM], [field, half] + faces, "prep", stream, grant=52
    )(place, current.reshape(cube))
    got = exchange(*sent)
    (w,) = call(
        table_kernel, [VMEM] * 4, [shape((8 * nodes, 256), BF16)], "tables", [pltpu.VMEM((128, 128), F32)]
    )(place, *small)
    *views, rh, rl = call(
        functools.partial(both_kernel, nx, ny), [VMEM] * 3, [packed] * 6, "both"
    )(v, r, small[2])
    pack = call(functools.partial(pack_kernel, nx, ny), [VMEM], [packed] * 4, "pack")
    scratch = [pltpu.VMEM((n, 16, nz), BF16) for n in (ny, ny, ny, ny, nx, nx, nx, nx)]
    v, *sent = call(
        functools.partial(sweep_kernel, nx, ny, False),
        [VMEM] * 15, [field, half] + faces, "sweep_a", scratch,
    )(place, w, cls, v, rh, rl, *views, *got)
    got = exchange(*sent)
    views = pack(v)
    (out,) = call(
        functools.partial(sweep_kernel, nx, ny, True),
        [VMEM] * 15, [shape(cube, F32)], "sweep_b", stream + [pltpu.VMEM((nx * ny * nodes, nz), F32)] + scratch, streamed=True,
    )(place, w, cls, v, rh, rl, *views, *got)
    return out.reshape(current.shape)


def solution(mesh):
    placed = (
        P("tm", None, "sx", "sy", None),
        P("tm", None, "sx", "sy", None),
        P("tm", "sx", "sy", None),
        P(),
        P(),
        P(),
    )
    return jax.shard_map(
        on_device,
        mesh=mesh,
        in_specs=placed,
        out_specs=P("tm", None, "sx", "sy", None),
        check_vma=False,
    )
```
